256 devices in a mesh: feat: 128 (over z, y, x), dp: 2 (over core).
Axes of the slice: x: 4, y: 4, z: 8, core: 2. Of those that a mesh axis runs over, the one named last changes fastest.
Arguments:
- grad_emb: bfloat16 [4096, 128, 128], P(('dp', 'feat')), may hold values from -0.59765625 to 0.59765625
- ids: int32 [4096, 128], P('dp', 'feat'), may hold values from 0 to 32767
- seeds: int32 [2, 1024], replicated, may hold values from 1 to 65520
- w_in: bfloat16 [128, 1024, 1024], P('feat'), may hold values from -0.1875 to 0.1875
- w_out: bfloat16 [128, 1024, 128], P('feat'), may hold values from -0.1875 to 0.1875
Outputs:
- grad_w_in: float32 [128, 1024, 1024], P('feat', None, 'dp')
- grad_w_out: float32 [128, 1024, 128], P('feat', 'dp')
The draws below stay inside these ranges and needn't reach their ends.
All inputs are finite; a program needn't handle non-finite values.
Results may differ from the reference program's by a relative error of at most 0.004.
Values may be sent and summed in bfloat16 or wider, within the bound.
A program may use at most 64 MiB of HBM per device.

```python
import math
import jax
import jax.numpy as jnp
import numpy as np
from jax import lax

K = 1024
H = 1024
E = 128
VOCAB = 32768
FEATS = 128
SAMPLES = 4096


def place_ends(drawn, stream_key, smallest, largest):
    shape = drawn.shape
    index_at = [jax.random.randint(jax.random.fold_in(stream_key, axis), (), 0, shape[axis]) for axis in range(len(shape))]
    drawn = drawn.at[tuple(index_at)].set(smallest)
    longest = shape.index(max(shape))
    index_at[longest] = (index_at[longest] + 1) % shape[longest]
    return drawn.at[tuple(index_at)].set(largest)


def levels(key, extent, split, smallest, high):
    def one(dim, blocks):
        steps = jax.random.uniform(jax.random.fold_in(jax.random.fold_in(key, 6), dim), (blocks,), jnp.float32, smallest / len(split), high / len(split))
        return jnp.repeat(jnp.exp(steps), extent[dim] // blocks).reshape((-1,) + (1,) * (len(extent) - dim - 1))

    level = one(*split[0])
    for cut in split[1:]:
        level = level * one(*cut)
    return level


def rank_table(count, lean):
    loads = [(1 << 20) // math.isqrt(grade ** lean) + 1 for grade in range(1, count + 1)]
    deviation = 1 + sum(loads) // (1 << 30)
    return np.cumsum(np.array([max(1, weight // deviation) for weight in loads]))


def skewed_ids(stream_key, extent, number_of, skew):
    grid = rank_table(number_of, skew)
    lot = jax.random.randint(jax.random.fold_in(stream_key, 1), extent, 0, int(grid[number_of - 1]))
    grade = jnp.searchsorted(jnp.asarray(grid, jnp.int32), lot, side="right")
    return jax.random.permutation(jax.random.fold_in(stream_key, 2), number_of)[grade].astype(jnp.int32)


def centred(rng, extent, deviation, bound, pieces=(), kind=jnp.bfloat16):
    result = deviation * jax.random.normal(rng, extent, jnp.float32)
    if pieces:
        result = result * levels(rng, extent, pieces, -0.22, 0.18)
    return jnp.clip(result, -bound, bound).astype(kind)


def setup_inputs(seed: int = 0) -> dict:
    arg_keys = jax.random.split(jax.random.key(seed), 6)
    grad_emb = centred(arg_keys[0], (SAMPLES, FEATS, E), 0.1, 0.59765625, ((0, 256),))
    ids = place_ends(skewed_ids(arg_keys[1], (SAMPLES, FEATS), VOCAB, 2), jax.random.fold_in(arg_keys[1], 3), 0, VOCAB - 1).astype(jnp.int32)
    seeds = place_ends(jax.random.randint(arg_keys[2], (2, K), 1, 65521), jax.random.fold_in(arg_keys[2], 1), 1, 65520).astype(jnp.int32)
    w_in = centred(arg_keys[3], (FEATS, K, H), K ** -0.5, 0.1875, ((0, 128),))
    w_out = centred(arg_keys[4], (FEATS, H, E), H ** -0.5, 0.1875, ((0, 128),))
    return dict(grad_emb=grad_emb, ids=ids, seeds=seeds, w_in=w_in, w_out=w_out)


prime_mod = 65521


def encode(id_col, seeds):
    hashed = jnp.remainder(id_col[:, None] * seeds[0][None, :] + seeds[1][None, :], prime_mod)
    return (hashed.astype(jnp.float32) * (2.0 / (prime_mod - 1)) - 1.0).astype(jnp.bfloat16)


def mish(value):
    return value * jnp.tanh(jax.nn.softplus(value))


def mish_slope(value):
    squash = jnp.tanh(jax.nn.softplus(value))
    return squash + value * (1.0 - squash * squash) * jax.nn.sigmoid(value)


def reference(grad_emb, ids, seeds, w_in, w_out):
    def one_feature(feature):
        encoding = encode(ids[:, feature], seeds)
        pre = jnp.dot(encoding, w_in[feature], preferred_element_type=jnp.float32)
        hidden = mish(pre).astype(jnp.bfloat16)
        upper = grad_emb[:, feature, :]
        back_hidden = jnp.dot(upper, w_out[feature].T, preferred_element_type=jnp.float32)
        back_pre = (back_hidden * mish_slope(pre)).astype(jnp.bfloat16)
        grad_first = jnp.dot(encoding.T, back_pre, preferred_element_type=jnp.float32)
        grad_last = jnp.dot(hidden.T, upper, preferred_element_type=jnp.float32)
        return grad_first, grad_last

    grad_w_in, grad_w_out = lax.map(one_feature, jnp.arange(FEATS, dtype=jnp.int32))
    return grad_w_in, grad_w_out
```

```python
import functools

import jax
import jax.numpy as jnp
from jax import lax
from jax.experimental import pallas as pl
from jax.experimental.pallas import tpu as pltpu
from jax.sharding import PartitionSpec as P

PRIME = 65521
HALF = 32760
MESH = pl.DeviceIdType.MESH
NX, NY, NZ = 4, 4, 8
FEATS = 128
ROWS = 16
K = 1024
H2 = 512
E = 128
HC = 512
F32 = jnp.float32
BF16 = jnp.bfloat16


def place():
    me = lax.axis_index("feat")
    return me, me // (NX * NY), (me // NX) % NY, me % NX


def target(step):
    _, mz, my, mx = place()
    plane, hop = step // NZ, step % NZ
    dz = jnp.where(hop % 2 == 1, (hop + 1) // 2, (NZ - hop // 2) % NZ)
    dy, dx = plane // NX, plane % NX
    z, y, x = (mz + dz) % NZ, (my + dy) % NY, (mx + dx) % NX
    return z * (NX * NY) + y * NX + x, dy


def fold(x):
    r = (x >> 16) * 15 + (x & 65535)
    return jnp.where(r >= PRIME, r - PRIME, r)


def coefficient_rows(seeds):
    a, b = seeds[0:1, :], seeds[1:2, :]
    a1, a2 = fold(a * 32), fold(a * 1024)
    shift = fold(b + 16 * (a + a1 + a2) + (PRIME - HALF))
    rows = []
    for c in (a, a1, a2, shift):
        c = jnp.where(c > HALF, c - PRIME, c)
        high = (c + 128) >> 8
        rows += [high * 256, c - high * 256]
    rows.append(jnp.zeros((128 - len(rows), K), jnp.int32))
    return jnp.concatenate(rows, axis=0).astype(F32)


def digits(ids, out, base):
    lane = lax.broadcasted_iota(jnp.int32, (1, 128), 1)
    row = lax.broadcasted_iota(jnp.int32, (16, 128), 0)
    turned = pltpu.roll(ids, 64, 1)
    for y in range(NY):
        for m in range(NZ // 2):
            r0 = 4 * m + y // 2
            r1 = r0 + 2
            first, second = (ids, turned) if y % 2 == 0 else (turned, ids)
            line = jnp.where(lane < 64, first[r0 : r0 + 1, :], second[r1 : r1 + 1, :])
            wide = jnp.broadcast_to(line, (16, 128))
            digit = ((wide >> ((row >> 1) * 5)) & 31) - 16
            digit = jnp.where(row < 6, digit, jnp.where(row < 8, 1, 0))
            out[2 * y + base, :, m * 128 : (m + 1) * 128] = digit.astype(F32).astype(BF16)


def nt(left, right):
    return lax.dot_general(left, right, (((1,), (1,)), ((), ())), preferred_element_type=F32)


def kernel(
    g_hbm, ids_hbm, seeds_hbm, win_hbm, wout_hbm, gin_hbm, gout_hbm,
    g_v, g_f, send, upper, ids_v, seeds_v, win_v, winT, wout_v, coef, digit, enc, pre, hid, slope, acc, acc_o,
    load, out_sem, send_sem, recv_sem, ids_send, ids_recv, pass_send, pass_recv,
):
    me, mz, my, mx = place()
    core = lax.axis_index("dp")
    sibling = {"dp": 1 - core}
    loads = [
        pltpu.make_async_copy(g_hbm, g_v, load.at[0]),
        pltpu.make_async_copy(ids_hbm, ids_v.at[0], load.at[1]),
        pltpu.make_async_copy(seeds_hbm, seeds_v, load.at[2]),
        pltpu.make_async_copy(win_hbm.at[0, :, pl.ds(pl.multiple_of(core * H2, H2), H2)], win_v, load.at[3]),
        pltpu.make_async_copy(wout_hbm.at[0, pl.ds(pl.multiple_of(core * H2, H2), H2), :], wout_v, load.at[4]),
    ]
    for c in loads:
        c.start()

    barrier = pltpu.get_barrier_semaphore()

    @pl.loop(1, FEATS)
    def _(i):
        pl.semaphore_signal(barrier, inc=1, device_id={"feat": (me + i) % FEATS}, device_id_type=MESH)

    pl.semaphore_signal(barrier, inc=1, device_id=sibling, device_id_type=MESH)

    loads[0].wait()
    g_f[...] = g_v[...].astype(F32).reshape(ROWS * FEATS, E)

    @pl.loop(0, FEATS, unroll=8)
    def _(f):
        send[f] = g_f[pl.ds(f, ROWS, stride=FEATS), :].astype(BF16)

    slot = my * (NZ * NX) + mz * NX + mx
    upper[0, slot] = send[me]
    loads[1].wait()
    pl.semaphore_wait(barrier, FEATS)

    ids_copy = pltpu.make_async_remote_copy(
        src_ref=ids_v.at[0], dst_ref=ids_v.at[1], send_sem=ids_send, recv_sem=ids_recv,
        device_id=sibling, device_id_type=MESH,
    )
    ids_copy.start()

    @pl.loop(1, FEATS)
    def _(i):
        to, dy = target(i)
        pltpu.make_async_remote_copy(
            src_ref=send.at[to], dst_ref=upper.at[0, slot], send_sem=send_sem, recv_sem=recv_sem.at[dy],
            device_id={"feat": to}, device_id_type=MESH,
        ).start()

    loads[2].wait()
    coef[...] = jnp.transpose(coefficient_rows(seeds_v[...]))[:, :16].astype(BF16)
    loads[3].wait()
    for b in range(K // 128):
        winT[:, b * 128 : (b + 1) * 128] = jnp.transpose(win_v[b * 128 : (b + 1) * 128, :].astype(F32)).astype(BF16)
    digits(ids_v[0], digit, 0)
    ids_copy.wait()
    digits(ids_v[1], digit, 1)

    @pl.loop(0, 8)
    def _(i):
        for r in range(0, K, 256):
            w = jnp.dot(coef[r : r + 256, :], digit[i], preferred_element_type=F32)
            turns = jnp.round(w * F32(1.0 / PRIME))
            enc[i, r : r + 256, :] = ((w - turns * F32(PRIME)) * F32(2.0 / (PRIME - 1))).astype(BF16)
        pre[...] = jnp.dot(winT[...], enc[i], preferred_element_type=F32)
        for r in range(0, H2, 32):
            v = pre[r : r + 32, :]
            e = jnp.exp(jnp.minimum(v, 20.0))
            square = e * e
            half = 0.5 * square + e
            both = square + e
            inv = 1.0 / (half + 1.0)
            u = v * inv
            hid[i, r : r + 32, :] = (half * u).astype(BF16)
            slope[i, r : r + 32, :] = (half + both * u) * inv

    loads[4].wait()
    acc[...] = jnp.zeros_like(acc)
    acc_o[...] = jnp.zeros_like(acc_o)

    def part(y, side):
        i = 2 * y + side
        up = upper[side, pl.ds(y * (NZ * NX), NZ * NX)].reshape(HC, E)
        back = nt(wout_v[...], up)
        back_pre = (back * slope[i]).astype(BF16)
        acc_o[...] += jnp.dot(hid[i], up, preferred_element_type=F32)
        acc[...] += nt(enc[i], back_pre)

    def received(dy, y, count):
        first = y * (NZ * NX)
        return pltpu.make_async_remote_copy(
            src_ref=send.at[pl.ds(0, count)], dst_ref=upper.at[0, pl.ds(first, count)], send_sem=send_sem,
            recv_sem=recv_sem.at[dy], device_id=sibling, device_id_type=MESH,
        )

    def passed(dy, y):
        first = y * (NZ * NX)
        return pltpu.make_async_remote_copy(
            src_ref=upper.at[0, pl.ds(first, NZ * NX)], dst_ref=upper.at[1, pl.ds(first, NZ * NX)],
            send_sem=pass_send.at[dy], recv_sem=pass_recv.at[dy], device_id=sibling, device_id_type=MESH,
        )

    @pl.loop(0, NY)
    def _(dy):
        y = (my - dy + NY) % NY

        @pl.when(dy == 0)
        def _():
            received(dy, y, NZ * NX - 1).wait_recv()

        @pl.when(dy > 0)
        def _():
            received(dy, y, NZ * NX).wait_recv()

        onward = passed(dy, y)
        onward.start()
        part(y, 0)
        onward.wait()
        part(y, 1)

    outs = [
        pltpu.make_async_copy(acc, gin_hbm.at[0], out_sem.at[0]),
        pltpu.make_async_copy(acc_o, gout_hbm.at[0], out_sem.at[1]),
    ]
    for c in outs:
        c.start()
    pltpu.make_async_remote_copy(
        src_ref=send.at[pl.ds(0, FEATS - 1)], dst_ref=upper.at[0, pl.ds(0, FEATS - 1)], send_sem=send_sem,
        recv_sem=recv_sem.at[0], device_id=sibling, device_id_type=MESH,
    ).wait_send()
    for c in outs:
        c.wait()


def on_device(grad_emb, ids, seeds, w_in, w_out):
    dma = pltpu.SemaphoreType.DMA
    gin, gout = pl.pallas_call(
        kernel,
        out_shape=(jax.ShapeDtypeStruct((1, K, H2), F32), jax.ShapeDtypeStruct((1, H2, E), F32)),
        in_specs=[pl.BlockSpec(memory_space=pl.ANY)] * 5,
        out_specs=[pl.BlockSpec(memory_space=pl.ANY)] * 2,
        scratch_shapes=[
            pltpu.VMEM((ROWS, FEATS, E), BF16),
            pltpu.VMEM((ROWS * FEATS, E), F32),
            pltpu.VMEM((FEATS, ROWS, E), BF16),
            pltpu.VMEM((2, FEATS, ROWS, E), BF16),
            pltpu.VMEM((2, 16, 128), jnp.int32),
            pltpu.VMEM((2, K), jnp.int32),
            pltpu.VMEM((K, H2), BF16),
            pltpu.VMEM((H2, K), BF16),
            pltpu.VMEM((H2, E), BF16),
            pltpu.VMEM((K, 16), BF16),
            pltpu.VMEM((8, 16, HC), BF16),
            pltpu.VMEM((8, K, HC), BF16),
            pltpu.VMEM((H2, HC), F32),
            pltpu.VMEM((8, H2, HC), BF16),
            pltpu.VMEM((8, H2, HC), F32),
            pltpu.VMEM((K, H2), F32),
            pltpu.VMEM((H2, E), F32),
            dma((5,)), dma((2,)), dma, dma((NY,)), dma, dma, dma((NY,)), dma((NY,)),
        ],
        compiler_params=pltpu.CompilerParams(
            collective_id=0, has_side_effects=True, vmem_limit_bytes=56 * 2**20
        ),
        name="feature_backward",
    )(grad_emb, ids.reshape(16, 128), seeds, w_in, w_out)
    return gin, gout


def solution(mesh):
    return jax.shard_map(
        on_device,
        mesh=mesh,
        in_specs=(
            P(("dp", "feat"), None, None),
            P("dp", "feat"),
            P(),
            P("feat", None, None),
            P("feat", None, None),
        ),
        out_specs=(P("feat", None, "dp"), P("feat", "dp", None)),
        check_vma=False,
    )
```

```python
import functools

import jax
import jax.numpy as jnp
from jax import lax
from jax.experimental import pallas as pl
from jax.experimental.pallas import tpu as pltpu
from jax.sharding import PartitionSpec as P

PRIME = 65521
HALF = 32760
ONE = 2**21
MESH = pl.DeviceIdType.MESH
NX, NY, NZ = 4, 4, 8
FEATS = 128
ROWS = 16
K = 1024
H2 = 512
E = 128
HC = 512
F32 = jnp.float32
BF16 = jnp.bfloat16


def place():
    me = lax.axis_index("feat")
    return me, me // (NX * NY), (me // NX) % NY, me % NX


def wrap(value, size):
    return jnp.where(value >= size, value - size, value)


def fold(x):
    return (x >> 16) * 15 + (x & 65535)


def coefficient_rows(seeds):
    row = lax.broadcasted_iota(jnp.int32, (16, K), 0)
    shift = jnp.broadcast_to(seeds[1:2, :] + (PRIME - HALF), (16, K))
    x = fold(fold(jnp.where(row < 15, jnp.broadcast_to(seeds[0:1, :], (16, K)) << row, shift)))
    x = jnp.where(x >= PRIME, x - PRIME, x)
    x = jnp.where(x > HALF, x - PRIME, x)
    fixed = jnp.round(x.astype(F32) * F32(ONE / PRIME)).astype(jnp.int32)
    high = (fixed + 8192) >> 14
    rest = fixed - (high << 14)
    middle = (rest + 64) >> 7
    parts = [high << 14, middle << 7, rest - (middle << 7)]
    rows = [p.astype(F32) * F32(1.0 / ONE) for p in parts]
    return jnp.concatenate(rows + [jnp.zeros((128 - 48, K), F32)], axis=0)


def bits(ids, out, base):
    lane = lax.broadcasted_iota(jnp.int32, (1, 128), 1)
    row = lax.broadcasted_iota(jnp.int32, (16, 128), 0)
    turned = pltpu.roll(ids, 64, 1)
    for y in range(NY):
        for m in range(NZ // 2):
            r0 = 4 * m + y // 2
            r1 = r0 + 2
            first, second = (ids, turned) if y % 2 == 0 else (turned, ids)
            line = jnp.where(lane < 64, first[r0 : r0 + 1, :], second[r1 : r1 + 1, :])
            wide = jnp.broadcast_to(line, (16, 128))
            bit = jnp.where(row < 15, (wide >> row) & 1, 1).astype(F32).astype(BF16)
            for r in range(0, 48, 16):
                out[2 * y + base, r : r + 16, m * 128 : (m + 1) * 128] = bit


def nt(left, right):
    return lax.dot_general(left, right, (((1,), (1,)), ((), ())), preferred_element_type=F32)


def kernel(
    g_hbm, ids_hbm, seeds_hbm, win_hbm, wout_hbm, acc, acc_o,
    g_v, g_f, send, upper, ids_v, seeds_v, win_v, winT, wout_v, coef, digit, enc_a, enc_b, pre_a, pre_b, hid, slope,
    load, send_sem, recv_sem, ids_send, ids_recv, pass_send, pass_recv,
):
    me, mz, my, mx = place()
    core = lax.axis_index("dp")
    sibling = {"dp": 1 - core}
    loads = [
        pltpu.make_async_copy(g_hbm, g_v, load.at[0]),
        pltpu.make_async_copy(ids_hbm, ids_v.at[0], load.at[1]),
        pltpu.make_async_copy(seeds_hbm, seeds_v, load.at[2]),
        pltpu.make_async_copy(win_hbm.at[0, :, pl.ds(pl.multiple_of(core * H2, H2), H2)], win_v, load.at[3]),
        pltpu.make_async_copy(wout_hbm.at[0, pl.ds(pl.multiple_of(core * H2, H2), H2), :], wout_v, load.at[4]),
    ]
    for c in loads:
        c.start()

    barrier = pltpu.get_barrier_semaphore()

    @pl.loop(0, FEATS - 1, unroll=True)
    def _(i):
        other = jnp.where(i >= me, i + 1, i)
        pl.semaphore_signal(barrier, inc=1, device_id={"feat": other}, device_id_type=MESH)

    pl.semaphore_signal(barrier, inc=1, device_id=sibling, device_id_type=MESH)

    loads[0].wait()
    g_f[...] = g_v[...].astype(F32).reshape(ROWS * FEATS, E)

    @pl.loop(0, FEATS, unroll=8)
    def _(f):
        send[f] = g_f[pl.ds(f, ROWS, stride=FEATS), :].astype(BF16)

    slot = my * (NZ * NX) + mz * NX + mx
    upper[0, slot] = send[me]
    loads[1].wait()
    pl.semaphore_wait(barrier, FEATS)

    ids_copy = pltpu.make_async_remote_copy(
        src_ref=ids_v.at[0], dst_ref=ids_v.at[1], send_sem=ids_send, recv_sem=ids_recv,
        device_id=sibling, device_id_type=MESH,
    )
    ids_copy.start()

    columns = [wrap(mz + dz, NZ) * (NX * NY) for dz in (0, 1, 7, 2, 6, 3, 5, 4)]

    def send_to(to, dy):
        pltpu.make_async_remote_copy(
            src_ref=send.at[to], dst_ref=upper.at[0, slot], send_sem=send_sem, recv_sem=recv_sem.at[dy],
            device_id={"feat": to}, device_id_type=MESH,
        ).start()

    @pl.loop(0, NY)
    def _(dy):
        y = wrap(my + dy, NY) * NX

        @pl.loop(0, NX)
        def _(dx):
            near = y + wrap(mx + dx, NX)

            @pl.when(dy + dx > 0)
            def _():
                send_to(columns[0] + near, dy)

            for column in columns[1:]:
                send_to(column + near, dy)

    loads[2].wait()
    coef[...] = jnp.transpose(coefficient_rows(seeds_v[...]))[:, :48].astype(BF16)
    loads[3].wait()
    for b in range(K // 128):
        winT[:, b * 128 : (b + 1) * 128] = jnp.transpose(win_v[b * 128 : (b + 1) * 128, :].astype(F32)).astype(BF16)
    bits(ids_v[0], digit, 0)
    ids_copy.wait()
    bits(ids_v[1], digit, 1)

    def encode(out, j, i):
        for r in range(0, K, 256):
            w = jnp.dot(coef[r : r + 256, :], digit[i], preferred_element_type=F32)
            out[j, r : r + 256, :] = ((w - jnp.round(w)) * F32(2.0 * PRIME / (PRIME - 1))).astype(BF16)

    def forward(block, out):
        out[...] = jnp.dot(winT[...], block, preferred_element_type=F32)

    def activate(pre, i):
        for r in range(0, H2, 16):
            v = pre[r : r + 16, :]
            e = jnp.exp(jnp.minimum(v, 20.0))
            square = e * e
            half = 0.5 * square + e
            both = square + e
            inv = 1.0 / (half + 1.0)
            u = v * inv
            hid[i, r : r + 16, :] = (half * u).astype(BF16)
            slope[i, r : r + 16, :] = (half + both * u) * inv

    encode(enc_a, 0, 0)
    pre_b[...] = jnp.zeros_like(pre_b)

    @pl.loop(0, NY)
    def _(j):
        forward(enc_a[j], pre_a)
        encode(enc_b, j, 2 * j + 1)
        activate(pre_b, (2 * j + 7) % 8)
        forward(enc_b[j], pre_b)
        encode(enc_a, (j + 1) % NY, (2 * j + 2) % 8)
        activate(pre_a, 2 * j)

    activate(pre_b, 7)
    loads[4].wait()
    acc[...] = jnp.zeros_like(acc)
    acc_o[...] = jnp.zeros_like(acc_o)

    def part(y, side):
        i = 2 * y + side
        up = upper[side, pl.ds(y * (NZ * NX), NZ * NX)].reshape(HC, E)
        back = nt(wout_v[...], up)
        back_pre = (back * slope[i]).astype(BF16)
        acc_o[0] += jnp.dot(hid[i], up, preferred_element_type=F32)
        acc[0] += nt((enc_a, enc_b)[side][y], back_pre)

    def received(dy, y, count):
        first = y * (NZ * NX)
        return pltpu.make_async_remote_copy(
            src_ref=send.at[pl.ds(0, count)], dst_ref=upper.at[0, pl.ds(first, count)], send_sem=send_sem,
            recv_sem=recv_sem.at[dy], device_id=sibling, device_id_type=MESH,
        )

    def passed(dy, y):
        first = y * (NZ * NX)
        return pltpu.make_async_remote_copy(
            src_ref=upper.at[0, pl.ds(first, NZ * NX)], dst_ref=upper.at[1, pl.ds(first, NZ * NX)],
            send_sem=pass_send.at[dy], recv_sem=pass_recv.at[dy], device_id=sibling, device_id_type=MESH,
        )

    @pl.loop(0, NY)
    def _(dy):
        y = (my - dy + NY) % NY

        @pl.when(dy == 0)
        def _():
            received(dy, y, NZ * NX - 1).wait_recv()

        @pl.when(dy > 0)
        def _():
            received(dy, y, NZ * NX).wait_recv()

        onward = passed(dy, y)
        onward.start()
        part(y, 0)
        onward.wait()
        part(y, 1)

    pltpu.make_async_remote_copy(
        src_ref=send.at[pl.ds(0, FEATS - 1)], dst_ref=upper.at[0, pl.ds(0, FEATS - 1)], send_sem=send_sem,
        recv_sem=recv_sem.at[0], device_id=sibling, device_id_type=MESH,
    ).wait_send()


def write_out(acc, acc_o, gin_hbm, gout_hbm, sem):
    copies = [
        pltpu.make_async_copy(acc, gin_hbm, sem.at[0]),
        pltpu.make_async_copy(acc_o, gout_hbm, sem.at[1]),
    ]
    for c in copies:
        c.start()
    for c in copies:
        c.wait()


def on_device(grad_emb, ids, seeds, w_in, w_out):
    dma = pltpu.SemaphoreType.DMA
    sums = pl.pallas_call(
        kernel,
        out_shape=(pltpu.VMEM((1, K, H2), F32), pltpu.VMEM((1, H2, E), F32)),
        in_specs=[pl.BlockSpec(memory_space=pl.ANY)] * 5,
        out_specs=[pl.BlockSpec(memory_space=pltpu.VMEM)] * 2,
        scratch_shapes=[
            pltpu.VMEM((ROWS, FEATS, E), BF16),
            pltpu.VMEM((ROWS * FEATS, E), F32),
            pltpu.VMEM((FEATS, ROWS, E), BF16),
            pltpu.VMEM((2, FEATS, ROWS, E), BF16),
            pltpu.VMEM((2, 16, 128), jnp.int32),
            pltpu.VMEM((2, K), jnp.int32),
            pltpu.VMEM((K, H2), BF16),
            pltpu.VMEM((H2, K), BF16),
            pltpu.VMEM((H2, E), BF16),
            pltpu.VMEM((K, 48), BF16),
            pltpu.VMEM((8, 48, HC), BF16),
            pltpu.VMEM((NY, K, HC), BF16),
            pltpu.VMEM((NY, K, HC), BF16),
            pltpu.VMEM((H2, HC), F32),
            pltpu.VMEM((H2, HC), F32),
            pltpu.VMEM((8, H2, HC), BF16),
            pltpu.VMEM((8, H2, HC), F32),
            dma((5,)), dma, dma((NY,)), dma, dma, dma((NY,)), dma((NY,)),
        ],
        compiler_params=pltpu.CompilerParams(
            collective_id=0, has_side_effects=True, vmem_limit_bytes=48 * 2**20
        ),
        name="feature_backward",
    )(*[
        pltpu.with_memory_space_constraint(x, pltpu.HBM)
        for x in (grad_emb, ids.reshape(16, 128), seeds, w_in, w_out)
    ])
    return pl.pallas_call(
        write_out,
        out_shape=(pltpu.HBM((1, K, H2), F32), pltpu.HBM((1, H2, E), F32)),
        in_specs=[pl.BlockSpec(memory_space=pltpu.VMEM)] * 2,
        out_specs=[pl.BlockSpec(memory_space=pltpu.HBM)] * 2,
        scratch_shapes=[dma((2,))],
        name="write_out",
    )(*[pltpu.with_memory_space_constraint(x, pltpu.VMEM) for x in sums])


def solution(mesh):
    return jax.shard_map(
        on_device,
        mesh=mesh,
        in_specs=(
            P(("dp", "feat"), None, None),
            P("dp", "feat"),
            P(),
            P("feat", None, None),
            P("feat", None, None),
        ),
        out_specs=(P("feat", None, "dp"), P("feat", "dp", None)),
        check_vma=False,
    )
```

```python
import functools

import jax
import jax.numpy as jnp
from jax import lax
from jax.experimental import pallas as pl
from jax.experimental.pallas import tpu as pltpu
from jax.sharding import PartitionSpec as P

PRIME = 65521
HALF = 32760
ONE = 2**21
MESH = pl.DeviceIdType.MESH
NX, NY, NZ = 4, 4, 8
FEATS = 128
ROWS = 16
K = 1024
H2 = 512
E = 128
HC = 512
F32 = jnp.float32
BF16 = jnp.bfloat16


def place():
    me = lax.axis_index("feat")
    return me, me // (NX * NY), (me // NX) % NY, me % NX


def wrap(value, size):
    return jnp.where(value >= size, value - size, value)


def fold(x):
    return (x >> 16) * 15 + (x & 65535)


def coefficient_rows(seeds):
    row = lax.broadcasted_iota(jnp.int32, (16, K), 0)
    shift = jnp.broadcast_to(seeds[1:2, :] + (PRIME - HALF), (16, K))
    x = fold(fold(jnp.where(row < 15, jnp.broadcast_to(seeds[0:1, :], (16, K)) << row, shift)))
    x = jnp.where(x >= PRIME, x - PRIME, x)
    x = jnp.where(x > HALF, x - PRIME, x)
    fixed = jnp.round(x.astype(F32) * F32(ONE / PRIME)).astype(jnp.int32)
    high = (fixed + 8192) >> 14
    rest = fixed - (high << 14)
    middle = (rest + 64) >> 7
    parts = [high << 14, middle << 7, rest - (middle << 7)]
    rows = [p.astype(F32) * F32(1.0 / ONE) for p in parts]
    return jnp.concatenate(rows + [jnp.zeros((128 - 48, K), F32)], axis=0)


def bits(ids, out, side):
    lane = lax.broadcasted_iota(jnp.int32, (1, 128), 1)
    row = lax.broadcasted_iota(jnp.int32, (16, 128), 0)
    turned = [ids] + [pltpu.roll(ids, ROWS * t, 1) for t in range(1, 8)]
    for y in range(NY):
        for x in range(NX):
            line = jnp.zeros((1, 128), jnp.int32)
            for z in range(NZ):
                r = 2 * z + y // 2
                piece = turned[(z - 4 * (y % 2) - x) % 8][r : r + 1, :]
                line = jnp.where(lane // ROWS == z, piece, line)
            wide = jnp.broadcast_to(line, (16, 128))
            bit = jnp.where(row < 15, (wide >> row) & 1, 1).astype(F32).astype(BF16)
            for r in range(0, 48, 16):
                out[NY * side + y, r : r + 16, x * 128 : (x + 1) * 128] = bit


def nt(left, right):
    return lax.dot_general(left, right, (((1,), (1,)), ((), ())), preferred_element_type=F32)


def kernel(
    g_hbm, ids_hbm, seeds_hbm, win_hbm, wout_hbm, acc, acc_o, enc, last,
    g_v, g_f, send, upper, ids_v, seeds_v, win_v, winT, wout_v, coef, bit, enc_a, enc_b, pre_a, pre_b, hid, slope,
    load, send_sem, recv_sem, ids_send, ids_recv, pass_send, pass_recv,
):
    me, mz, my, mx = place()
    core = lax.axis_index("dp")
    sibling = {"dp": 1 - core}
    loads = [
        pltpu.make_async_copy(g_hbm, g_v, load.at[0]),
        pltpu.make_async_copy(ids_hbm, ids_v.at[0], load.at[1]),
        pltpu.make_async_copy(seeds_hbm, seeds_v, load.at[2]),
        pltpu.make_async_copy(win_hbm.at[0, :, pl.ds(pl.multiple_of(core * H2, H2), H2)], win_v, load.at[3]),
        pltpu.make_async_copy(wout_hbm.at[0, pl.ds(pl.multiple_of(core * H2, H2), H2), :], wout_v, load.at[4]),
    ]
    for c in loads:
        c.start()

    barrier = pltpu.get_barrier_semaphore()

    @pl.loop(0, FEATS - 1, unroll=True)
    def _(i):
        other = jnp.where(i >= me, i + 1, i)
        pl.semaphore_signal(barrier, inc=1, device_id={"feat": other}, device_id_type=MESH)

    pl.semaphore_signal(barrier, inc=1, device_id=sibling, device_id_type=MESH)

    loads[0].wait()
    g_f[...] = g_v[...].astype(F32).reshape(ROWS * FEATS, E)

    @pl.loop(0, FEATS, unroll=8)
    def _(f):
        send[f] = g_f[pl.ds(f, ROWS, stride=FEATS), :].astype(BF16)

    slot = my * (NX * NZ) + mx * NZ + mz
    upper[0, slot] = send[me]
    loads[1].wait()

    ids_copy = pltpu.make_async_remote_copy(
        src_ref=ids_v.at[0], dst_ref=ids_v.at[1], send_sem=ids_send, recv_sem=ids_recv,
        device_id=sibling, device_id_type=MESH,
    )
    columns = [wrap(mz + dz, NZ) * (NX * NY) for dz in (0, 1, 7, 2, 6, 3, 5, 4)]

    def send_to(to, dy):
        pltpu.make_async_remote_copy(
            src_ref=send.at[to], dst_ref=upper.at[0, slot], send_sem=send_sem, recv_sem=recv_sem.at[dy],
            device_id={"feat": to}, device_id_type=MESH,
        ).start()

    def communicate():
        pl.semaphore_wait(barrier, FEATS)
        ids_copy.start()

        @pl.loop(0, NY)
        def _(dy):
            y = wrap(my + dy, NY) * NX

            @pl.loop(0, NX)
            def _(dx):
                near = y + wrap(mx + dx, NX)

                @pl.when(dy + dx > 0)
                def _():
                    send_to(columns[0] + near, dy)

                for column in columns[1:]:
                    send_to(column + near, dy)

    def home(q):
        return wrap(my - q + NY, NY)

    def encode(out, b):
        side = jnp.where(b >= NY, 1, 0)
        i = NY * side + home(b - NY * side)
        for r in range(0, K, 256):
            w = jnp.dot(coef[r : r + 256, :], bit[i], preferred_element_type=F32)
            code = ((w - jnp.round(w)) * F32(2.0 * PRIME / (PRIME - 1))).astype(BF16)
            out[r : r + 256, :] = code
            enc[b, r : r + 256, :] = code

    def forward(block, out):
        out[...] = jnp.dot(winT[...], block[...], preferred_element_type=F32)

    def activate(pre, b):
        for r in range(0, H2, 16):
            v = pre[r : r + 16, :]
            e = jnp.exp(jnp.minimum(v, 20.0))
            square = e * e
            half = 0.5 * square + e
            both = square + e
            inv = 1.0 / (half + 1.0)
            u = v * inv
            hid[b, r : r + 16, :] = (half * u).astype(BF16)
            slope[b, r : r + 16, :] = (half + both * u) * inv

    def prepare():
        loads[2].wait()
        coef[...] = jnp.transpose(coefficient_rows(seeds_v[...]))[:, :48].astype(BF16)
        loads[3].wait()
        for b in range(K // 128):
            winT[:, b * 128 : (b + 1) * 128] = jnp.transpose(win_v[b * 128 : (b + 1) * 128, :].astype(F32)).astype(BF16)
        bits(ids_v[0], bit, 0)
        encode(enc_a, 0)
        pre_b[...] = jnp.zeros_like(pre_b)

    def pair(j):
        @pl.when(j == 0)
        def _():
            prepare()

        @pl.when(j == 1)
        def _():
            ids_copy.wait()
            bits(ids_v[1], bit, 1)

        forward(enc_a, pre_a)
        encode(enc_b, 2 * j + 1)
        activate(pre_b, (2 * j + 7) % 8)
        forward(enc_b, pre_b)
        encode(enc_a, (2 * j + 2) % 8)
        activate(pre_a, 2 * j)

    turn = jnp.where(me < FEATS // 2, 1, 0)

    @pl.loop(0, NY + 1)
    def _(step):
        @pl.when(step == turn)
        def _():
            communicate()

        @pl.when(step != turn)
        def _():
            pair(jnp.where(step > turn, step - 1, step))

    activate(pre_b, 7)
    loads[4].wait()
    acc[...] = jnp.zeros_like(acc)
    acc_o[...] = jnp.zeros_like(acc_o)

    def received(q, count):
        first = home(q) * (NX * NZ)
        return pltpu.make_async_remote_copy(
            src_ref=send.at[pl.ds(0, count)], dst_ref=upper.at[0, pl.ds(first, count)], send_sem=send_sem,
            recv_sem=recv_sem.at[q], device_id=sibling, device_id_type=MESH,
        )

    def passed(q):
        first = home(q) * (NX * NZ)
        return pltpu.make_async_remote_copy(
            src_ref=upper.at[0, pl.ds(first, NX * NZ)], dst_ref=upper.at[1, pl.ds(first, NX * NZ)],
            send_sem=pass_send.at[q], recv_sem=pass_recv.at[q], device_id=sibling, device_id_type=MESH,
        )

    def arrive(q, count=NX * NZ):
        received(q, count).wait_recv()
        passed(q).start()

    def back(q, side):
        b = NY * side + q
        up = upper[side, pl.ds(home(q) * (NX * NZ), NX * NZ)].reshape(HC, E)
        back_pre = (nt(wout_v[...], up) * slope[b]).astype(BF16)
        acc_o[0] += jnp.dot(hid[b], up, preferred_element_type=F32)
        return back_pre

    def part(q, side):
        back_pre = back(q, side)
        acc[0] += nt(enc[NY * side + q], back_pre)

    arrive(0, NX * NZ - 1)

    @pl.loop(0, NY)
    def _(q):
        part(q, 0)

        @pl.when(q < NY - 2)
        def _():
            arrive(q + 1)

        @pl.when(q < NY - 1)
        def _():
            passed(q).wait()
            part(q, 1)

        @pl.when(q == NY - 2)
        def _():
            arrive(q + 1)

    passed(NY - 1).wait()
    last[...] = back(NY - 1, 1)
    pltpu.make_async_remote_copy(
        src_ref=send.at[pl.ds(0, FEATS - 1)], dst_ref=upper.at[0, pl.ds(0, FEATS - 1)], send_sem=send_sem,
        recv_sem=recv_sem.at[0], device_id=sibling, device_id_type=MESH,
    ).wait_send()


def finish(acc, acc_o, enc, last, gin_hbm, gout_hbm, total, sem):
    small = pltpu.make_async_copy(acc_o, gout_hbm, sem.at[0])
    small.start()
    copies = []
    for n, r in enumerate(range(0, K, 256)):
        total[r : r + 256, :] = acc[0, r : r + 256, :] + nt(enc[2 * NY - 1, r : r + 256, :], last[...])
        copy = pltpu.make_async_copy(total.at[pl.ds(r, 256)], gin_hbm.at[0, pl.ds(r, 256)], sem.at[n + 1])
        copy.start()
        copies.append(copy)
    for copy in copies:
        copy.wait()
    small.wait()


def on_device(grad_emb, ids, seeds, w_in, w_out):
    dma = pltpu.SemaphoreType.DMA
    sums = pl.pallas_call(
        kernel,
        out_shape=(
            pltpu.VMEM((1, K, H2), F32),
            pltpu.VMEM((1, H2, E), F32),
            pltpu.VMEM((2 * NY, K, HC), BF16),
            pltpu.VMEM((H2, HC), BF16),
        ),
        in_specs=[pl.BlockSpec(memory_space=pl.ANY)] * 5,
        out_specs=[pl.BlockSpec(memory_space=pltpu.VMEM)] * 4,
        scratch_shapes=[
            pltpu.VMEM((ROWS, FEATS, E), BF16),
            pltpu.VMEM((ROWS * FEATS, E), F32),
            pltpu.VMEM((FEATS, ROWS, E), BF16),
            pltpu.VMEM((2, FEATS, ROWS, E), BF16),
            pltpu.VMEM((2, 16, 128), jnp.int32),
            pltpu.VMEM((2, K), jnp.int32),
            pltpu.VMEM((K, H2), BF16),
            pltpu.VMEM((H2, K), BF16),
            pltpu.VMEM((H2, E), BF16),
            pltpu.VMEM((K, 48), BF16),
            pltpu.VMEM((2 * NY, 48, HC), BF16),
            pltpu.VMEM((K, HC), BF16),
            pltpu.VMEM((K, HC), BF16),
            pltpu.VMEM((H2, HC), F32),
            pltpu.VMEM((H2, HC), F32),
            pltpu.VMEM((2 * NY, H2, HC), BF16),
            pltpu.VMEM((2 * NY, H2, HC), F32),
            dma((5,)), dma, dma((NY,)), dma, dma, dma((NY,)), dma((NY,)),
        ],
        compiler_params=pltpu.CompilerParams(
            collective_id=0, has_side_effects=True, vmem_limit_bytes=40 * 2**20
        ),
        name="feature_backward",
    )(*[
        pltpu.with_memory_space_constraint(x, pltpu.HBM)
        for x in (grad_emb, ids.reshape(16, 128), seeds, w_in, w_out)
    ])
    return pl.pallas_call(
        finish,
        out_shape=(pltpu.HBM((1, K, H2), F32), pltpu.HBM((1, H2, E), F32)),
        in_specs=[pl.BlockSpec(memory_space=pltpu.VMEM)] * 4,
        out_specs=[pl.BlockSpec(memory_space=pltpu.HBM)] * 2,
        scratch_shapes=[pltpu.VMEM((K, H2), F32), dma((5,))],
        compiler_params=pltpu.CompilerParams(vmem_limit_bytes=8 * 2**20),
        name="finish",
    )(*[pltpu.with_memory_space_constraint(x, pltpu.VMEM) for x in sums])


def solution(mesh):
    return jax.shard_map(
        on_device,
        mesh=mesh,
        in_specs=(
            P(("dp", "feat"), None, None),
            P("dp", "feat"),
            P(),
            P("feat", None, None),
            P("feat", None, None),
        ),
        out_specs=(P("feat", None, "dp"), P("feat", "dp", None)),
        check_vma=False,
    )
```

```python
import functools

import jax
import jax.numpy as jnp
from jax import lax
from jax.experimental import pallas as pl
from jax.experimental.pallas import tpu as pltpu
from jax.sharding import PartitionSpec as P

PRIME = 65521
HALF = 32760
ONE = 2**21
MESH = pl.DeviceIdType.MESH
NX, NY, NZ = 4, 4, 8
FEATS = 128
ROWS = 16
K = 1024
H2 = 512
E = 128
HC = 512
F32 = jnp.float32
BF16 = jnp.bfloat16


def place():
    me = lax.axis_index("feat")
    return me, me // (NX * NY), (me // NX) % NY, me % NX


def wrap(value, size):
    return jnp.where(value >= size, value - size, value)


def far_first(q):
    return jnp.where(q == 0, 2, jnp.where(q == 1, 1, jnp.where(q == 2, 3, 0)))


def fold(x):
    return (x >> 16) * 15 + (x & 65535)


def coefficient_rows(seeds):
    row = lax.broadcasted_iota(jnp.int32, (16, K), 0)
    shift = jnp.broadcast_to(seeds[1:2, :] + (PRIME - HALF), (16, K))
    x = fold(fold(jnp.where(row < 15, jnp.broadcast_to(seeds[0:1, :], (16, K)) << row, shift)))
    x = jnp.where(x >= PRIME, x - PRIME, x)
    x = jnp.where(x > HALF, x - PRIME, x)
    fixed = jnp.round(x.astype(F32) * F32(ONE / PRIME)).astype(jnp.int32)
    high = (fixed + 8192) >> 14
    rest = fixed - (high << 14)
    middle = (rest + 64) >> 7
    parts = [high << 14, middle << 7, rest - (middle << 7)]
    rows = [p.astype(F32) * F32(1.0 / ONE) for p in parts]
    return jnp.concatenate(rows + [jnp.zeros((128 - 48, K), F32)], axis=0)


def bits(ids, out, side):
    lane = lax.broadcasted_iota(jnp.int32, (1, 128), 1)
    row = lax.broadcasted_iota(jnp.int32, (16, 128), 0)
    turned = [ids] + [pltpu.roll(ids, ROWS * t, 1) for t in range(1, 8)]
    for y in range(NY):
        for x in range(NX):
            line = jnp.zeros((1, 128), jnp.int32)
            for z in range(NZ):
                r = 2 * z + y // 2
                piece = turned[(z - 4 * (y % 2) - x) % 8][r : r + 1, :]
                line = jnp.where(lane // ROWS == z, piece, line)
            wide = jnp.broadcast_to(line, (16, 128))
            bit = jnp.where(row < 15, (wide >> row) & 1, 1).astype(F32).astype(BF16)
            for r in range(0, 48, 16):
                out[NY * side + y, r : r + 16, x * 128 : (x + 1) * 128] = bit


def nt(left, right):
    return lax.dot_general(left, right, (((1,), (1,)), ((), ())), preferred_element_type=F32)


def kernel(
    g_hbm, ids_hbm, seeds_hbm, win_hbm, wout_hbm, acc, acc_o, enc, last,
    g_v, g_f, send, upper, ids_v, seeds_v, win_v, winT, wout_v, coef, bit, enc_a, enc_b, pre_a, pre_b, hid, slope,
    load, send_sem, recv_sem, ids_send, ids_recv, pass_send, pass_recv,
):
    me, mz, my, mx = place()
    core = lax.axis_index("dp")
    sibling = {"dp": 1 - core}
    loads = [
        pltpu.make_async_copy(g_hbm, g_v, load.at[0]),
        pltpu.make_async_copy(ids_hbm, ids_v.at[0], load.at[1]),
        pltpu.make_async_copy(seeds_hbm, seeds_v, load.at[2]),
        pltpu.make_async_copy(win_hbm.at[0, :, pl.ds(pl.multiple_of(core * H2, H2), H2)], win_v, load.at[3]),
        pltpu.make_async_copy(wout_hbm.at[0, pl.ds(pl.multiple_of(core * H2, H2), H2), :], wout_v, load.at[4]),
    ]
    for c in loads:
        c.start()

    barrier = pltpu.get_barrier_semaphore()

    @pl.loop(0, FEATS - 1)
    def _(i):
        other = jnp.where(i >= me, i + 1, i)
        pl.semaphore_signal(barrier, inc=1, device_id={"feat": other}, device_id_type=MESH)

    pl.semaphore_signal(barrier, inc=1, device_id=sibling, device_id_type=MESH)

    loads[0].wait()
    g_f[...] = g_v[...].astype(F32).reshape(ROWS * FEATS, E)

    @pl.loop(0, FEATS, unroll=8)
    def _(f):
        send[f] = g_f[pl.ds(f, ROWS, stride=FEATS), :].astype(BF16)

    slot = my * (NX * NZ) + mx * NZ + mz
    upper[0, slot] = send[me]
    loads[1].wait()

    ids_copy = pltpu.make_async_remote_copy(
        src_ref=ids_v.at[0], dst_ref=ids_v.at[1], send_sem=ids_send, recv_sem=ids_recv,
        device_id=sibling, device_id_type=MESH,
    )
    columns = [wrap(mz + dz, NZ) * (NX * NY) for dz in (4, 3, 5, 2, 6, 1, 7, 0)]

    def send_to(to, q):
        pltpu.make_async_remote_copy(
            src_ref=send.at[to], dst_ref=upper.at[0, slot], send_sem=send_sem, recv_sem=recv_sem.at[q],
            device_id={"feat": to}, device_id_type=MESH,
        ).start()

    def communicate():
        pl.semaphore_wait(barrier, FEATS)
        ids_copy.start()

        @pl.loop(0, NY)
        def _(q):
            y = wrap(my + far_first(q), NY) * NX

            @pl.loop(0, NX)
            def _(p):
                near = y + wrap(mx + far_first(p), NX)
                for column in columns[:-1]:
                    send_to(column + near, q)

                @pl.when(q + p < NY + NX - 2)
                def _():
                    send_to(columns[-1] + near, q)

    def home(q):
        return wrap(my - far_first(q) + NY, NY)

    def encode(out, b):
        side = jnp.where(b >= NY, 1, 0)
        i = NY * side + home(b - NY * side)
        for r in range(0, K, 256):
            w = jnp.dot(coef[r : r + 256, :], bit[i], preferred_element_type=F32)
            code = ((w - jnp.round(w)) * F32(2.0 * PRIME / (PRIME - 1))).astype(BF16)
            out[r : r + 256, :] = code
            enc[b, r : r + 256, :] = code

    def forward(block, out):
        out[...] = jnp.dot(winT[...], block[...], preferred_element_type=F32)

    def activate(pre, b):
        for r in range(0, H2, 16):
            v = pre[r : r + 16, :]
            e = jnp.exp(jnp.minimum(v, 20.0))
            square = e * e
            half = 0.5 * square + e
            both = square + e
            inv = 1.0 / (half + 1.0)
            u = v * inv
            hid[b, r : r + 16, :] = (half * u).astype(BF16)
            slope[b, r : r + 16, :] = (half + both * u) * inv

    def prepare():
        loads[2].wait()
        coef[...] = jnp.transpose(coefficient_rows(seeds_v[...]))[:, :48].astype(BF16)
        loads[3].wait()
        for b in range(K // 128):
            winT[:, b * 128 : (b + 1) * 128] = jnp.transpose(win_v[b * 128 : (b + 1) * 128, :].astype(F32)).astype(BF16)
        bits(ids_v[0], bit, 0)
        encode(enc_a, 0)
        pre_b[...] = jnp.zeros_like(pre_b)

    def pair(j):
        @pl.when(j == 0)
        def _():
            prepare()

        @pl.when(j == 1)
        def _():
            ids_copy.wait()
            bits(ids_v[1], bit, 1)

        forward(enc_a, pre_a)
        encode(enc_b, 2 * j + 1)
        activate(pre_b, (2 * j + 7) % 8)
        forward(enc_b, pre_b)
        encode(enc_a, (2 * j + 2) % 8)
        activate(pre_a, 2 * j)

    turn = jnp.where(me < FEATS // 2, 1, 0)

    @pl.loop(0, NY + 1)
    def _(step):
        @pl.when(step == turn)
        def _():
            communicate()

        @pl.when(step != turn)
        def _():
            pair(jnp.where(step > turn, step - 1, step))

    activate(pre_b, 7)
    loads[4].wait()
    acc[...] = jnp.zeros_like(acc)
    acc_o[...] = jnp.zeros_like(acc_o)

    def received(q, count):
        first = home(q) * (NX * NZ)
        return pltpu.make_async_remote_copy(
            src_ref=send.at[pl.ds(0, count)], dst_ref=upper.at[0, pl.ds(first, count)], send_sem=send_sem,
            recv_sem=recv_sem.at[q], device_id=sibling, device_id_type=MESH,
        )

    def passed(q):
        first = home(q) * (NX * NZ)
        return pltpu.make_async_remote_copy(
            src_ref=upper.at[0, pl.ds(first, NX * NZ)], dst_ref=upper.at[1, pl.ds(first, NX * NZ)],
            send_sem=pass_send.at[q], recv_sem=pass_recv.at[q], device_id=sibling, device_id_type=MESH,
        )

    def arrive(q, count):
        received(q, count).wait_recv()
        passed(q).start()

    def back(q, side):
        b = NY * side + q
        up = upper[side, pl.ds(home(q) * (NX * NZ), NX * NZ)].reshape(HC, E)
        back_pre = (nt(wout_v[...], up) * slope[b]).astype(BF16)
        acc_o[0] += jnp.dot(hid[b], up, preferred_element_type=F32)
        return back_pre

    def part(q, side):
        back_pre = back(q, side)
        acc[0] += nt(enc[NY * side + q], back_pre)

    arrive(0, NX * NZ)

    @pl.loop(0, NY - 1)
    def _(q):
        part(q, 0)

        @pl.when(q < NY - 2)
        def _():
            arrive(q + 1, NX * NZ)

        @pl.when(q == NY - 2)
        def _():
            arrive(q + 1, NX * NZ - 1)

        passed(q).wait()
        part(q, 1)

    part(NY - 1, 0)
    passed(NY - 1).wait()
    last[...] = back(NY - 1, 1)
    pltpu.make_async_remote_copy(
        src_ref=send.at[pl.ds(0, FEATS - 1)], dst_ref=upper.at[0, pl.ds(0, FEATS - 1)], send_sem=send_sem,
        recv_sem=recv_sem.at[0], device_id=sibling, device_id_type=MESH,
    ).wait_send()


def finish(acc, acc_o, enc, last, gin_hbm, gout_hbm, total, sem):
    small = pltpu.make_async_copy(acc_o, gout_hbm, sem.at[0])
    small.start()
    copies = []
    for n, r in enumerate(range(0, K, 256)):
        total[r : r + 256, :] = acc[0, r : r + 256, :] + nt(enc[2 * NY - 1, r : r + 256, :], last[...])
        copy = pltpu.make_async_copy(total.at[pl.ds(r, 256)], gin_hbm.at[0, pl.ds(r, 256)], sem.at[n + 1])
        copy.start()
        copies.append(copy)
    for copy in copies:
        copy.wait()
    small.wait()


def on_device(grad_emb, ids, seeds, w_in, w_out):
    dma = pltpu.SemaphoreType.DMA
    sums = pl.pallas_call(
        kernel,
        out_shape=(
            pltpu.VMEM((1, K, H2), F32),
            pltpu.VMEM((1, H2, E), F32),
            pltpu.VMEM((2 * NY, K, HC), BF16),
            pltpu.VMEM((H2, HC), BF16),
        ),
        in_specs=[pl.BlockSpec(memory_space=pl.ANY)] * 5,
        out_specs=[pl.BlockSpec(memory_space=pltpu.VMEM)] * 4,
        scratch_shapes=[
            pltpu.VMEM((ROWS, FEATS, E), BF16),
            pltpu.VMEM((ROWS * FEATS, E), F32),
            pltpu.VMEM((FEATS, ROWS, E), BF16),
            pltpu.VMEM((2, FEATS, ROWS, E), BF16),
            pltpu.VMEM((2, 16, 128), jnp.int32),
            pltpu.VMEM((2, K), jnp.int32),
            pltpu.VMEM((K, H2), BF16),
            pltpu.VMEM((H2, K), BF16),
            pltpu.VMEM((H2, E), BF16),
            pltpu.VMEM((K, 48), BF16),
            pltpu.VMEM((2 * NY, 48, HC), BF16),
            pltpu.VMEM((K, HC), BF16),
            pltpu.VMEM((K, HC), BF16),
            pltpu.VMEM((H2, HC), F32),
            pltpu.VMEM((H2, HC), F32),
            pltpu.VMEM((2 * NY, H2, HC), BF16),
            pltpu.VMEM((2 * NY, H2, HC), F32),
            dma((5,)), dma, dma((NY,)), dma, dma, dma((NY,)), dma((NY,)),
        ],
        compiler_params=pltpu.CompilerParams(
            collective_id=0, has_side_effects=True, vmem_limit_bytes=40 * 2**20
        ),
        name="feature_backward",
    )(*[
        pltpu.with_memory_space_constraint(x, pltpu.HBM)
        for x in (grad_emb, ids.reshape(16, 128), seeds, w_in, w_out)
    ])
    return pl.pallas_call(
        finish,
        out_shape=(pltpu.HBM((1, K, H2), F32), pltpu.HBM((1, H2, E), F32)),
        in_specs=[pl.BlockSpec(memory_space=pltpu.VMEM)] * 4,
        out_specs=[pl.BlockSpec(memory_space=pltpu.HBM)] * 2,
        scratch_shapes=[pltpu.VMEM((K, H2), F32), dma((5,))],
        compiler_params=pltpu.CompilerParams(vmem_limit_bytes=8 * 2**20),
        name="finish",
    )(*[pltpu.with_memory_space_constraint(x, pltpu.VMEM) for x in sums])


def solution(mesh):
    return jax.shard_map(
        on_device,
        mesh=mesh,
        in_specs=(
            P(("dp", "feat"), None, None),
            P("dp", "feat"),
            P(),
            P("feat", None, None),
            P("feat", None, None),
        ),
        out_specs=(P("feat", None, "dp"), P("feat", "dp", None)),
        check_vma=False,
    )
```

```python
import functools

import jax
import jax.numpy as jnp
from jax import lax
from jax.experimental import pallas as pl
from jax.experimental.pallas import tpu as pltpu
from jax.sharding import PartitionSpec as P

PRIME = 65521
HALF = 32760
ONE = 2**21
MESH = pl.DeviceIdType.MESH
NX, NY, NZ = 4, 4, 8
FEATS = 128
ROWS = 16
K = 1024
H2 = 512
E = 128
HC = 512
F32 = jnp.float32
BF16 = jnp.bfloat16


def place():
    me = lax.axis_index("feat")
    return me, me // (NX * NY), (me // NX) % NY, me % NX


def wrap(value, size):
    return jnp.where(value >= size, value - size, value)


def far_first(q):
    return jnp.where(q == 0, 2, jnp.where(q == 1, 1, jnp.where(q == 2, 3, 0)))


def fold(x):
    return (x >> 16) * 15 + (x & 65535)


def coefficient_rows(seeds):
    row = lax.broadcasted_iota(jnp.int32, (16, K), 0)
    shift = jnp.broadcast_to(seeds[1:2, :] + (PRIME - HALF), (16, K))
    x = fold(fold(jnp.where(row < 15, jnp.broadcast_to(seeds[0:1, :], (16, K)) << row, shift)))
    x = jnp.where(x >= PRIME, x - PRIME, x)
    x = jnp.where(x > HALF, x - PRIME, x)
    fixed = jnp.round(x.astype(F32) * F32(ONE / PRIME)).astype(jnp.int32)
    high = (fixed + 8192) >> 14
    rest = fixed - (high << 14)
    middle = (rest + 64) >> 7
    parts = [high << 14, middle << 7, rest - (middle << 7)]
    rows = [p.astype(F32) * F32(1.0 / ONE) for p in parts]
    return jnp.concatenate(rows + [jnp.zeros((128 - 48, K), F32)], axis=0)


def bits(ids, out, side):
    lane = lax.broadcasted_iota(jnp.int32, (1, 128), 1)
    row = lax.broadcasted_iota(jnp.int32, (16, 128), 0)
    turned = [ids] + [pltpu.roll(ids, ROWS * t, 1) for t in range(1, 8)]
    for y in range(NY):
        for x in range(NX):
            line = jnp.zeros((1, 128), jnp.int32)
            for z in range(NZ):
                r = 2 * z + y // 2
                piece = turned[(z - 4 * (y % 2) - x) % 8][r : r + 1, :]
                line = jnp.where(lane // ROWS == z, piece, line)
            wide = jnp.broadcast_to(line, (16, 128))
            bit = jnp.where(row < 15, (wide >> row) & 1, 1).astype(F32).astype(BF16)
            for r in range(0, 48, 16):
                out[NY * side + y, r : r + 16, x * 128 : (x + 1) * 128] = bit


def nt(left, right):
    return lax.dot_general(left, right, (((1,), (1,)), ((), ())), preferred_element_type=F32)


def kernel(
    g_hbm, ids_hbm, seeds_hbm, win_hbm, wout_hbm, acc, acc_o, enc, last,
    g_v, g_f, send, upper, ids_v, seeds_v, win_v, winT, wout_v, coef, bit, enc_a, enc_b, pre_a, pre_b, hid, slope,
    load, send_sem, recv_sem, ids_send, ids_recv, pass_send, pass_recv,
):
    me, mz, my, mx = place()
    core = lax.axis_index("dp")
    sibling = {"dp": 1 - core}
    loads = [
        pltpu.make_async_copy(g_hbm, g_v, load.at[0]),
        pltpu.make_async_copy(ids_hbm, ids_v.at[0], load.at[1]),
        pltpu.make_async_copy(seeds_hbm, seeds_v, load.at[2]),
        pltpu.make_async_copy(win_hbm.at[0, :, pl.ds(pl.multiple_of(core * H2, H2), H2)], win_v, load.at[3]),
        pltpu.make_async_copy(wout_hbm.at[0, pl.ds(pl.multiple_of(core * H2, H2), H2), :], wout_v, load.at[4]),
    ]
    for c in loads:
        c.start()

    barrier = pltpu.get_barrier_semaphore()

    @pl.loop(0, FEATS - 1, unroll=True)
    def _(i):
        other = jnp.where(i >= me, i + 1, i)
        pl.semaphore_signal(barrier, inc=1, device_id={"feat": other}, device_id_type=MESH)

    pl.semaphore_signal(barrier, inc=1, device_id=sibling, device_id_type=MESH)

    loads[0].wait()
    g_f[...] = g_v[...].astype(F32).reshape(ROWS * FEATS, E)

    @pl.loop(0, FEATS, unroll=8)
    def _(f):
        send[f] = g_f[pl.ds(f, ROWS, stride=FEATS), :].astype(BF16)

    slot = my * (NX * NZ) + mx * NZ + mz
    upper[0, slot] = send[me]
    loads[1].wait()

    ids_copy = pltpu.make_async_remote_copy(
        src_ref=ids_v.at[0], dst_ref=ids_v.at[1], send_sem=ids_send, recv_sem=ids_recv,
        device_id=sibling, device_id_type=MESH,
    )
    columns = [wrap(mz + dz, NZ) * (NX * NY) for dz in (4, 3, 5, 2, 6, 1, 7, 0)]

    def send_to(to, q):
        pltpu.make_async_remote_copy(
            src_ref=send.at[to], dst_ref=upper.at[0, slot], send_sem=send_sem, recv_sem=recv_sem.at[q],
            device_id={"feat": to}, device_id_type=MESH,
        ).start()

    def communicate():
        pl.semaphore_wait(barrier, FEATS)
        ids_copy.start()

        @pl.loop(0, NY)
        def _(q):
            y = wrap(my + far_first(q), NY) * NX

            @pl.loop(0, NX)
            def _(p):
                near = y + wrap(mx + far_first(p), NX)
                for column in columns[:-1]:
                    send_to(column + near, q)

                @pl.when(q + p < NY + NX - 2)
                def _():
                    send_to(columns[-1] + near, q)

    def home(q):
        return wrap(my - far_first(q) + NY, NY)

    def encode(out, b):
        side = jnp.where(b >= NY, 1, 0)
        i = NY * side + home(b - NY * side)
        for r in range(0, K, 256):
            w = jnp.dot(coef[r : r + 256, :], bit[i], preferred_element_type=F32)
            code = ((w - jnp.round(w)) * F32(2.0 * PRIME / (PRIME - 1))).astype(BF16)
            out[r : r + 256, :] = code
            enc[b, r : r + 256, :] = code

    def forward(block, out):
        out[...] = jnp.dot(winT[...], block[...], preferred_element_type=F32)

    def activate(pre, b):
        for r in range(0, H2, 16):
            v = pre[r : r + 16, :]
            e = jnp.exp(jnp.minimum(v, 20.0))
            square = e * e
            half = 0.5 * square + e
            both = square + e
            inv = 1.0 / (half + 1.0)
            u = v * inv
            hid[b, r : r + 16, :] = (half * u).astype(BF16)
            slope[b, r : r + 16, :] = (half + both * u) * inv

    turn = jnp.where(me < FEATS // 4, 2, jnp.where(me < FEATS // 2, 1, 0))

    def prepare():
        loads[2].wait()
        coef[...] = jnp.transpose(coefficient_rows(seeds_v[...]))[:, :48].astype(BF16)
        loads[3].wait()
        for b in range(K // 128):
            winT[:, b * 128 : (b + 1) * 128] = jnp.transpose(win_v[b * 128 : (b + 1) * 128, :].astype(F32)).astype(BF16)
        bits(ids_v[0], bit, 0)
        encode(enc_a, 0)
        pre_b[...] = jnp.zeros_like(pre_b)

    def pair(j):
        @pl.when(j == 0)
        def _():
            prepare()

        @pl.when(j == jnp.maximum(turn, 1))
        def _():
            ids_copy.wait_recv()
            bits(ids_v[1], bit, 1)

            @pl.when(j == 2)
            def _():
                encode(enc_a, NY)

        forward(enc_a, pre_a)
        encode(enc_b, 2 * j + 1)
        activate(pre_b, (2 * j + 7) % 8)
        forward(enc_b, pre_b)
        encode(enc_a, (2 * j + 2) % 8)
        activate(pre_a, 2 * j)

    @pl.loop(0, NY + 1)
    def _(step):
        @pl.when(step == turn)
        def _():
            communicate()

        @pl.when(step != turn)
        def _():
            pair(jnp.where(step > turn, step - 1, step))

    activate(pre_b, 7)
    loads[4].wait()
    acc[...] = jnp.zeros_like(acc)
    acc_o[...] = jnp.zeros_like(acc_o)

    def received(q, count):
        first = home(q) * (NX * NZ)
        return pltpu.make_async_remote_copy(
            src_ref=send.at[pl.ds(0, count)], dst_ref=upper.at[0, pl.ds(first, count)], send_sem=send_sem,
            recv_sem=recv_sem.at[q], device_id=sibling, device_id_type=MESH,
        )

    def passed(q):
        first = home(q) * (NX * NZ)
        return pltpu.make_async_remote_copy(
            src_ref=upper.at[0, pl.ds(first, NX * NZ)], dst_ref=upper.at[1, pl.ds(first, NX * NZ)],
            send_sem=pass_send.at[q], recv_sem=pass_recv.at[q], device_id=sibling, device_id_type=MESH,
        )

    def arrive(q, count):
        received(q, count).wait_recv()
        passed(q).start()

    def back(q, side):
        b = NY * side + q
        up = upper[side, pl.ds(home(q) * (NX * NZ), NX * NZ)].reshape(HC, E)
        back_pre = (nt(wout_v[...], up) * slope[b]).astype(BF16)
        acc_o[0] += jnp.dot(hid[b], up, preferred_element_type=F32)
        return back_pre

    def part(q, side):
        back_pre = back(q, side)
        acc[0] += nt(enc[NY * side + q], back_pre)

    arrive(0, NX * NZ)

    @pl.loop(0, NY - 1)
    def _(q):
        part(q, 0)

        @pl.when(q < NY - 2)
        def _():
            arrive(q + 1, NX * NZ)

        @pl.when(q == NY - 2)
        def _():
            arrive(q + 1, NX * NZ - 1)

        passed(q).wait_recv()
        part(q, 1)

    part(NY - 1, 0)
    passed(NY - 1).wait_recv()
    last[...] = back(NY - 1, 1)
    pltpu.make_async_remote_copy(
        src_ref=send.at[pl.ds(0, FEATS - 1)], dst_ref=upper.at[0, pl.ds(0, FEATS - 1)], send_sem=send_sem,
        recv_sem=recv_sem.at[0], device_id=sibling, device_id_type=MESH,
    ).wait_send()
    ids_copy.wait_send()
    for q in range(NY):
        passed(q).wait_send()


def finish(acc, acc_o, enc, last, gin_hbm, gout_hbm, total, sem):
    small = pltpu.make_async_copy(acc_o, gout_hbm, sem.at[0])
    small.start()
    copies = []
    for n, r in enumerate(range(0, K, 256)):
        total[r : r + 256, :] = acc[0, r : r + 256, :] + nt(enc[2 * NY - 1, r : r + 256, :], last[...])
        copy = pltpu.make_async_copy(total.at[pl.ds(r, 256)], gin_hbm.at[0, pl.ds(r, 256)], sem.at[n + 1])
        copy.start()
        copies.append(copy)
    for copy in copies:
        copy.wait()
    small.wait()


def on_device(grad_emb, ids, seeds, w_in, w_out):
    dma = pltpu.SemaphoreType.DMA
    sums = pl.pallas_call(
        kernel,
        out_shape=(
            pltpu.VMEM((1, K, H2), F32),
            pltpu.VMEM((1, H2, E), F32),
            pltpu.VMEM((2 * NY, K, HC), BF16),
            pltpu.VMEM((H2, HC), BF16),
        ),
        in_specs=[pl.BlockSpec(memory_space=pl.ANY)] * 5,
        out_specs=[pl.BlockSpec(memory_space=pltpu.VMEM)] * 4,
        scratch_shapes=[
            pltpu.VMEM((ROWS, FEATS, E), BF16),
            pltpu.VMEM((ROWS * FEATS, E), F32),
            pltpu.VMEM((FEATS, ROWS, E), BF16),
            pltpu.VMEM((2, FEATS, ROWS, E), BF16),
            pltpu.VMEM((2, 16, 128), jnp.int32),
            pltpu.VMEM((2, K), jnp.int32),
            pltpu.VMEM((K, H2), BF16),
            pltpu.VMEM((H2, K), BF16),
            pltpu.VMEM((H2, E), BF16),
            pltpu.VMEM((K, 48), BF16),
            pltpu.VMEM((2 * NY, 48, HC), BF16),
            pltpu.VMEM((K, HC), BF16),
            pltpu.VMEM((K, HC), BF16),
            pltpu.VMEM((H2, HC), F32),
            pltpu.VMEM((H2, HC), F32),
            pltpu.VMEM((2 * NY, H2, HC), BF16),
            pltpu.VMEM((2 * NY, H2, HC), F32),
            dma((5,)), dma, dma((NY,)), dma, dma, dma((NY,)), dma((NY,)),
        ],
        compiler_params=pltpu.CompilerParams(
            collective_id=0, has_side_effects=True, vmem_limit_bytes=40 * 2**20
        ),
        name="feature_backward",
    )(*[
        pltpu.with_memory_space_constraint(x, pltpu.HBM)
        for x in (grad_emb, ids.reshape(16, 128), seeds, w_in, w_out)
    ])
    return pl.pallas_call(
        finish,
        out_shape=(pltpu.HBM((1, K, H2), F32), pltpu.HBM((1, H2, E), F32)),
        in_specs=[pl.BlockSpec(memory_space=pltpu.VMEM)] * 4,
        out_specs=[pl.BlockSpec(memory_space=pltpu.HBM)] * 2,
        scratch_shapes=[pltpu.VMEM((K, H2), F32), dma((5,))],
        compiler_params=pltpu.CompilerParams(vmem_limit_bytes=8 * 2**20),
        name="finish",
    )(*[pltpu.with_memory_space_constraint(x, pltpu.VMEM) for x in sums])


def solution(mesh):
    return jax.shard_map(
        on_device,
        mesh=mesh,
        in_specs=(
            P(("dp", "feat"), None, None),
            P("dp", "feat"),
            P(),
            P("feat", None, None),
            P("feat", None, None),
        ),
        out_specs=(P("feat", None, "dp"), P("feat", "dp", None)),
        check_vma=False,
    )
```

```python
import functools

import jax
import jax.numpy as jnp
from jax import lax
from jax.experimental import pallas as pl
from jax.experimental.pallas import tpu as pltpu
from jax.sharding import PartitionSpec as P

PRIME = 65521
HALF = 32760
ONE = 2**21
MESH = pl.DeviceIdType.MESH
NX, NY, NZ = 4, 4, 8
FEATS = 128
ROWS = 16
K = 1024
H2 = 512
E = 128
HC = 512
FAR = (2, 1, 3, 0)
F32 = jnp.float32
BF16 = jnp.bfloat16


def place():
    me = lax.axis_index("feat")
    return me, me // (NX * NY), (me // NX) % NY, me % NX


def wrap(value, size):
    return jnp.where(value >= size, value - size, value)


def far_first(q):
    return jnp.where(q == 0, 2, jnp.where(q == 1, 1, jnp.where(q == 2, 3, 0)))


def fold(x):
    return (x >> 16) * 15 + (x & 65535)


def coefficient_rows(seeds):
    row = lax.broadcasted_iota(jnp.int32, (16, K), 0)
    shift = jnp.broadcast_to(seeds[1:2, :] + (PRIME - HALF), (16, K))
    x = fold(fold(jnp.where(row < 15, jnp.broadcast_to(seeds[0:1, :], (16, K)) << row, shift)))
    x = jnp.where(x >= PRIME, x - PRIME, x)
    x = jnp.where(x > HALF, x - PRIME, x)
    fixed = jnp.round(x.astype(F32) * F32(ONE / PRIME)).astype(jnp.int32)
    high = (fixed + 8192) >> 14
    rest = fixed - (high << 14)
    middle = (rest + 64) >> 7
    parts = [high << 14, middle << 7, rest - (middle << 7)]
    rows = [p.astype(F32) * F32(1.0 / ONE) for p in parts]
    return jnp.concatenate(rows + [jnp.zeros((128 - 48, K), F32)], axis=0)


def bits(ids, out, side):
    lane = lax.broadcasted_iota(jnp.int32, (1, 128), 1)
    row = lax.broadcasted_iota(jnp.int32, (16, 128), 0)
    turned = [ids] + [pltpu.roll(ids, ROWS * t, 1) for t in range(1, 8)]
    for y in range(NY):
        for x in range(NX):
            line = jnp.zeros((1, 128), jnp.int32)
            for z in range(NZ):
                r = 2 * z + y // 2
                piece = turned[(z - 4 * (y % 2) - x) % 8][r : r + 1, :]
                line = jnp.where(lane // ROWS == z, piece, line)
            wide = jnp.broadcast_to(line, (16, 128))
            bit = jnp.where(row < 15, (wide >> row) & 1, 1).astype(F32).astype(BF16)
            for r in range(0, 48, 16):
                out[NY * side + y, r : r + 16, x * 128 : (x + 1) * 128] = bit


def nt(left, right):
    return lax.dot_general(left, right, (((1,), (1,)), ((), ())), preferred_element_type=F32)


def kernel(
    g_hbm, ids_hbm, seeds_hbm, win_hbm, wout_hbm, acc, acc_o, enc, last,
    g_v, g_f, send, upper, ids_v, seeds_v, win_v, winT, wout_v, coef, bit, enc_a, enc_b, pre_a, pre_b, hid, slope,
    load, send_sem, recv_sem, ids_send, ids_recv, pass_send, pass_recv,
):
    me, mz, my, mx = place()
    core = lax.axis_index("dp")
    sibling = {"dp": 1 - core}
    loads = [
        pltpu.make_async_copy(g_hbm, g_v, load.at[0]),
        pltpu.make_async_copy(ids_hbm, ids_v.at[0], load.at[1]),
        pltpu.make_async_copy(seeds_hbm, seeds_v, load.at[2]),
        pltpu.make_async_copy(win_hbm.at[0, :, pl.ds(pl.multiple_of(core * H2, H2), H2)], win_v, load.at[3]),
        pltpu.make_async_copy(wout_hbm.at[0, pl.ds(pl.multiple_of(core * H2, H2), H2), :], wout_v, load.at[4]),
    ]
    for c in loads:
        c.start()

    barrier = pltpu.get_barrier_semaphore()
    columns = [wrap(mz + dz, NZ) * (NX * NY) for dz in (4, 3, 5, 2, 6, 1, 7, 0)]

    def greet(other):
        pl.semaphore_signal(barrier, inc=1, device_id={"feat": other}, device_id_type=MESH)

    for q in FAR:
        y = wrap(my + q, NY) * NX
        for p in FAR:
            near = y + wrap(mx + p, NX)
            for column in columns[:-1] if p + q == 0 else columns:
                greet(column + near)
    pl.semaphore_signal(barrier, inc=1, device_id=sibling, device_id_type=MESH)

    loads[0].wait()
    g_f[...] = g_v[...].astype(F32).reshape(ROWS * FEATS, E)

    @pl.loop(0, FEATS, unroll=8)
    def _(f):
        send[f] = g_f[pl.ds(f, ROWS, stride=FEATS), :].astype(BF16)

    slot = my * (NX * NZ) + mx * NZ + mz
    upper[0, slot] = send[me]
    loads[1].wait()

    ids_copy = pltpu.make_async_remote_copy(
        src_ref=ids_v.at[0], dst_ref=ids_v.at[1], send_sem=ids_send, recv_sem=ids_recv,
        device_id=sibling, device_id_type=MESH,
    )
    def send_to(to, q):
        pltpu.make_async_remote_copy(
            src_ref=send.at[to], dst_ref=upper.at[0, slot], send_sem=send_sem, recv_sem=recv_sem.at[q],
            device_id={"feat": to}, device_id_type=MESH,
        ).start()

    def communicate():
        pl.semaphore_wait(barrier, FEATS)
        ids_copy.start()

        @pl.loop(0, NY)
        def _(q):
            y = wrap(my + far_first(q), NY) * NX

            @pl.loop(0, NX)
            def _(p):
                near = y + wrap(mx + far_first(p), NX)
                for column in columns[:-1]:
                    send_to(column + near, q)

                @pl.when(q + p < NY + NX - 2)
                def _():
                    send_to(columns[-1] + near, q)

    def home(q):
        return wrap(my - far_first(q) + NY, NY)

    def encode(out, b):
        side = jnp.where(b >= NY, 1, 0)
        i = NY * side + home(b - NY * side)
        for r in range(0, K, 256):
            w = jnp.dot(coef[r : r + 256, :], bit[i], preferred_element_type=F32)
            code = ((w - jnp.round(w)) * F32(2.0 * PRIME / (PRIME - 1))).astype(BF16)
            out[r : r + 256, :] = code
            enc[b, r : r + 256, :] = code

    def forward(block, out):
        out[...] = jnp.dot(winT[...], block[...], preferred_element_type=F32)

    def activate(pre, b):
        for r in range(0, H2, 16):
            v = pre[r : r + 16, :]
            e = jnp.exp(jnp.minimum(v, 20.0))
            square = e * e
            half = 0.5 * square + e
            both = square + e
            inv = 1.0 / (half + 1.0)
            u = v * inv
            hid[b, r : r + 16, :] = (half * u).astype(BF16)
            slope[b, r : r + 16, :] = (half + both * u) * inv

    turn = jnp.where(me < FEATS * 3 // 16, 2, jnp.where(me < FEATS // 2, 1, 0))

    def prepare():
        loads[2].wait()
        coef[...] = jnp.transpose(coefficient_rows(seeds_v[...]))[:, :48].astype(BF16)
        loads[3].wait()
        for b in range(K // 128):
            winT[:, b * 128 : (b + 1) * 128] = jnp.transpose(win_v[b * 128 : (b + 1) * 128, :].astype(F32)).astype(BF16)
        bits(ids_v[0], bit, 0)
        encode(enc_a, 0)
        pre_b[...] = jnp.zeros_like(pre_b)

    def pair(j):
        @pl.when(j == 0)
        def _():
            prepare()

        @pl.when(j == jnp.maximum(turn, 1))
        def _():
            ids_copy.wait_recv()
            bits(ids_v[1], bit, 1)

            @pl.when(j == 2)
            def _():
                encode(enc_a, NY)

        forward(enc_a, pre_a)
        encode(enc_b, 2 * j + 1)
        activate(pre_b, (2 * j + 7) % 8)
        forward(enc_b, pre_b)
        encode(enc_a, (2 * j + 2) % 8)
        activate(pre_a, 2 * j)

    @pl.loop(0, NY + 1)
    def _(step):
        @pl.when(step == turn)
        def _():
            communicate()

        @pl.when(step != turn)
        def _():
            pair(jnp.where(step > turn, step - 1, step))

    activate(pre_b, 7)
    loads[4].wait()
    acc[...] = jnp.zeros_like(acc)
    acc_o[...] = jnp.zeros_like(acc_o)

    def received(q, count):
        first = home(q) * (NX * NZ)
        return pltpu.make_async_remote_copy(
            src_ref=send.at[pl.ds(0, count)], dst_ref=upper.at[0, pl.ds(first, count)], send_sem=send_sem,
            recv_sem=recv_sem.at[q], device_id=sibling, device_id_type=MESH,
        )

    def passed(q):
        first = home(q) * (NX * NZ)
        return pltpu.make_async_remote_copy(
            src_ref=upper.at[0, pl.ds(first, NX * NZ)], dst_ref=upper.at[1, pl.ds(first, NX * NZ)],
            send_sem=pass_send.at[q], recv_sem=pass_recv.at[q], device_id=sibling, device_id_type=MESH,
        )

    def arrive(q, count):
        received(q, count).wait_recv()
        passed(q).start()

    def back(q, side):
        b = NY * side + q
        up = upper[side, pl.ds(home(q) * (NX * NZ), NX * NZ)].reshape(HC, E)
        back_pre = (nt(wout_v[...], up) * slope[b]).astype(BF16)
        acc_o[0] += jnp.dot(hid[b], up, preferred_element_type=F32)
        return back_pre

    def part(q, side):
        back_pre = back(q, side)
        acc[0] += nt(enc[NY * side + q], back_pre)

    arrive(0, NX * NZ)

    @pl.loop(0, NY - 1)
    def _(q):
        part(q, 0)

        @pl.when(q < NY - 2)
        def _():
            arrive(q + 1, NX * NZ)

        @pl.when(q == NY - 2)
        def _():
            arrive(q + 1, NX * NZ - 1)

        passed(q).wait_recv()
        part(q, 1)

    part(NY - 1, 0)
    passed(NY - 1).wait_recv()
    last[...] = back(NY - 1, 1)
    pltpu.make_async_remote_copy(
        src_ref=send.at[pl.ds(0, FEATS - 1)], dst_ref=upper.at[0, pl.ds(0, FEATS - 1)], send_sem=send_sem,
        recv_sem=recv_sem.at[0], device_id=sibling, device_id_type=MESH,
    ).wait_send()
    ids_copy.wait_send()
    for q in range(NY):
        passed(q).wait_send()


def finish(acc, acc_o, enc, last, gin_hbm, gout_hbm, total, sem):
    small = pltpu.make_async_copy(acc_o, gout_hbm, sem.at[0])
    small.start()
    copies = []
    for n, r in enumerate(range(0, K, 256)):
        total[r : r + 256, :] = acc[0, r : r + 256, :] + nt(enc[2 * NY - 1, r : r + 256, :], last[...])
        copy = pltpu.make_async_copy(total.at[pl.ds(r, 256)], gin_hbm.at[0, pl.ds(r, 256)], sem.at[n + 1])
        copy.start()
        copies.append(copy)
    for copy in copies:
        copy.wait()
    small.wait()


def on_device(grad_emb, ids, seeds, w_in, w_out):
    dma = pltpu.SemaphoreType.DMA
    sums = pl.pallas_call(
        kernel,
        out_shape=(
            pltpu.VMEM((1, K, H2), F32),
            pltpu.VMEM((1, H2, E), F32),
            pltpu.VMEM((2 * NY, K, HC), BF16),
            pltpu.VMEM((H2, HC), BF16),
        ),
        in_specs=[pl.BlockSpec(memory_space=pl.ANY)] * 5,
        out_specs=[pl.BlockSpec(memory_space=pltpu.VMEM)] * 4,
        scratch_shapes=[
            pltpu.VMEM((ROWS, FEATS, E), BF16),
            pltpu.VMEM((ROWS * FEATS, E), F32),
            pltpu.VMEM((FEATS, ROWS, E), BF16),
            pltpu.VMEM((2, FEATS, ROWS, E), BF16),
            pltpu.VMEM((2, 16, 128), jnp.int32),
            pltpu.VMEM((2, K), jnp.int32),
            pltpu.VMEM((K, H2), BF16),
            pltpu.VMEM((H2, K), BF16),
            pltpu.VMEM((H2, E), BF16),
            pltpu.VMEM((K, 48), BF16),
            pltpu.VMEM((2 * NY, 48, HC), BF16),
            pltpu.VMEM((K, HC), BF16),
            pltpu.VMEM((K, HC), BF16),
            pltpu.VMEM((H2, HC), F32),
            pltpu.VMEM((H2, HC), F32),
            pltpu.VMEM((2 * NY, H2, HC), BF16),
            pltpu.VMEM((2 * NY, H2, HC), F32),
            dma((5,)), dma, dma((NY,)), dma, dma, dma((NY,)), dma((NY,)),
        ],
        compiler_params=pltpu.CompilerParams(
            collective_id=0, has_side_effects=True, vmem_limit_bytes=40 * 2**20
        ),
        name="feature_backward",
    )(*[
        pltpu.with_memory_space_constraint(x, pltpu.HBM)
        for x in (grad_emb, ids.reshape(16, 128), seeds, w_in, w_out)
    ])
    return pl.pallas_call(
        finish,
        out_shape=(pltpu.HBM((1, K, H2), F32), pltpu.HBM((1, H2, E), F32)),
        in_specs=[pl.BlockSpec(memory_space=pltpu.VMEM)] * 4,
        out_specs=[pl.BlockSpec(memory_space=pltpu.HBM)] * 2,
        scratch_shapes=[pltpu.VMEM((K, H2), F32), dma((5,))],
        compiler_params=pltpu.CompilerParams(vmem_limit_bytes=8 * 2**20),
        name="finish",
    )(*[pltpu.with_memory_space_constraint(x, pltpu.VMEM) for x in sums])


def solution(mesh):
    return jax.shard_map(
        on_device,
        mesh=mesh,
        in_specs=(
            P(("dp", "feat"), None, None),
            P("dp", "feat"),
            P(),
            P("feat", None, None),
            P("feat", None, None),
        ),
        out_specs=(P("feat", None, "dp"), P("feat", "dp", None)),
        check_vma=False,
    )
```
